512 devices in a mesh: member: 32 (over z, x_lo), space: 16 (over x_hi, y, core).
Axes of the slice: x: 4 (x_hi: 2, x_lo: 2; x = x_hi * 2 + x_lo), y: 4, z: 16, core: 2. Of those that a mesh axis runs over, the one named last changes fastest.
Arguments:
- perturb: bfloat16 [64, 2, 2, 1024, 3072], P('member', None, None, 'space'), may hold values from -6 to 6
- control: float32 [64, 2, 2, 128, 256], P('member', None, None, 'space'), may hold values from -6 to 6
- lat_basis: bfloat16 [1024, 128], P('space'), may hold values from -0.5 to 0.5
- lon_basis: bfloat16 [3072, 256], P('member'), may hold values from -0.375 to 0.375
- innovation: bfloat16 [2, 2, 1024, 3072], P(None, None, 'space', 'member'), may hold values from -6 to 6
- weights: bfloat16 [2, 2, 1024, 3072], P(None, None, 'space', 'member'), may hold values from 0.5 to 4
Outputs:
- increment: float32 [2, 2, 1024, 3072], P(None, None, 'space', 'member')
- gradient: float32 [64, 2, 2, 128, 256], P('member', None, None, 'space')
The draws below stay inside these ranges and needn't reach their ends.
All inputs are finite; a program needn't handle non-finite values.
Results may differ from the reference program's by a relative error of at most 0.01.
Values may be sent and summed in bfloat16 or wider, within the bound.
No kernel may reach another device: no remote copies, remote signals or barrier semaphores. Data moves between devices by JAX's collectives and lax.ppermute only.
A program may use at most 64 MiB of HBM per device.

```python
import math
import jax
import jax.numpy as jnp
from jax import lax

NLON = 3072
KX = 256
KY = 128
FIELDS = 2
LEVELS = 2
NLAT = 1024
MEMBERS = 64


def block_scale(rng, shape, pieces, least, top_value):
    level, own = 1.0, jax.random.fold_in(rng, 6)
    for position, parts in pieces:
        steps = jnp.exp(jax.random.uniform(jax.random.fold_in(own, position), (parts,), jnp.float32, least / len(pieces), top_value / len(pieces)))
        level = level * jnp.repeat(steps, shape[position] // parts).reshape([-1 if axis == position else 1 for axis in range(len(shape))])
    return level


def scatter_about(own_key, extent, deviation, most, shards=(), kind=jnp.bfloat16):
    level = block_scale(own_key, extent, shards, -0.22, 0.18) if shards else 1.0
    array = jax.random.normal(own_key, extent, jnp.float32) * deviation * level
    return jnp.minimum(jnp.maximum(array, -most), most).astype(kind)


def setup_inputs(seed: int = 0) -> dict:
    seeds = jax.random.split(jax.random.key(seed), 7)
    perturb = scatter_about(seeds[0], (MEMBERS, FIELDS, LEVELS, NLAT, NLON), 1.0, 6.0, ((0, 32), (3, 16)))
    control = scatter_about(seeds[1], (MEMBERS, FIELDS, LEVELS, KY, KX), 1.0, 6.0, ((0, 32), (3, 16)), jnp.float32)
    lat_basis = scatter_about(seeds[2], (NLAT, KY), KY ** -0.5, 0.5, ((0, 16),))
    lon_basis = scatter_about(seeds[3], (NLON, KX), KX ** -0.5, 0.375, ((0, 32),))
    innovation = scatter_about(seeds[4], (FIELDS, LEVELS, NLAT, NLON), 1.0, 6.0, ((2, 16), (3, 32)))
    weights = jnp.clip(jnp.exp(math.log(4.0) - 2.0794415 * jax.random.uniform(seeds[5], (FIELDS, LEVELS, NLAT, NLON), jnp.float32) ** block_scale(seeds[5], (FIELDS, LEVELS, NLAT, NLON), ((2, 16), (3, 32)), -0.2, 0.2)), 0.5, 4.0).astype(jnp.bfloat16)
    return {"perturb": perturb, "control": control, "lat_basis": lat_basis, "lon_basis": lon_basis, "innovation": innovation, "weights": weights}


def field_of(member_ctrl, lat_basis, lon_basis):
    lat_part = jnp.einsum('yk,flkx->flyx', lat_basis.astype(jnp.float32), member_ctrl.astype(jnp.float32)).astype(jnp.bfloat16)
    return jnp.einsum('flyx,nx->flyn', lat_part.astype(jnp.float32), lon_basis.astype(jnp.float32))

def reference(perturb, control, lat_basis, lon_basis, innovation, weights):
    factor = 1.0 / math.sqrt(MEMBERS - 1)
    control_b = control.astype(jnp.bfloat16)

    def accumulate(running, pair):
        member_pert, member_ctrl = pair
        local_field = field_of(member_ctrl, lat_basis, lon_basis)
        return (running + member_pert.astype(jnp.float32) * local_field, None)
    start = jnp.zeros((FIELDS, LEVELS, NLAT, NLON), jnp.float32)
    summed, unused = lax.scan(accumulate, start, (perturb, control_b))
    increment = summed * factor
    forcing = (weights.astype(jnp.float32) * (increment - innovation.astype(jnp.float32))).astype(jnp.bfloat16)

    def backward(pair):
        member_pert, member_ctrl = pair
        weighted = (member_pert.astype(jnp.float32) * forcing.astype(jnp.float32)).astype(jnp.bfloat16)
        lon_back = jnp.einsum('flyn,nx->flyx', weighted.astype(jnp.float32), lon_basis.astype(jnp.float32)).astype(jnp.bfloat16)
        projected = jnp.einsum('yk,flyx->flkx', lat_basis.astype(jnp.float32), lon_back.astype(jnp.float32))
        return member_ctrl + factor * projected
    gradient = lax.map(backward, (perturb, control))
    return (increment, gradient)
```

```python
import math

import jax
import jax.numpy as jnp
from jax import lax
from jax.experimental import pallas as pl
from jax.experimental.pallas import tpu as pltpu
from jax.sharding import PartitionSpec as P

NEAR, FAR = 4, 8
ORDER = (0, 4, 2, 6, 1, 5, 3, 7)
NEAR_GROUPS = [[NEAR * far + near for near in range(NEAR)] for far in range(FAR)]
FAR_GROUPS = [[NEAR * far + near for far in ORDER] for near in range(NEAR)]
CORE_GROUPS = [[2 * chip, 2 * chip + 1] for chip in range(8)]
F32, BF16 = jnp.float32, jnp.bfloat16


def place(far):
    return (far % 2) * 4 + (far // 2 % 2) * 2 + far // 4


def spread(x, axis, groups, size):
    out = lax.all_to_all(
        jnp.broadcast_to(x[None], (size, *x.shape)), axis, 0, 0, tiled=True, axis_index_groups=groups
    )
    return out


def lon_block(lon_ref):
    return jnp.concatenate([lon_ref[half, near, 0] for near in range(NEAR) for half in range(2)], axis=0)


def forward_kernel(perturb_ref, control_ref, lat_ref, lon_ref, out_ref, part_ref):
    @pl.when(pl.program_id(0) == 0)
    def _():
        lat_part = jnp.dot(lat_ref[...], control_ref[...], preferred_element_type=F32).astype(BF16)
        for g in range(8):
            part_ref[64 * g : 64 * g + 64, :] = lat_part[:, 256 * g : 256 * g + 256]

    field = lax.dot_general(
        part_ref[...], lon_block(lon_ref), (((1,), (1,)), ((), ())), preferred_element_type=F32
    )
    terms = perturb_ref[...].astype(F32) * field
    total = (terms[:256] + terms[256:]).T.astype(BF16)
    for near in range(NEAR):
        out_ref[near, 0] = total[96 * near : 96 * near + 96]


def forcing_kernel(factor, parts_ref, innovation_ref, weights_ref, increment_ref, forcing_ref):
    summed = jnp.sum(parts_ref[...].astype(F32), axis=0) * factor
    increment = summed.T
    increment_ref[...] = increment
    forcing = weights_ref[...].astype(F32) * (increment - innovation_ref[...].astype(F32))
    forcing = forcing.T.astype(BF16)
    for far in range(FAR):
        forcing_ref[far] = forcing


def backward_kernel(perturb_ref, forcing_ref, lat_ref, lon_ref, out_ref, total_ref):
    step = pl.program_id(0)

    @pl.when(step == 0)
    def _():
        total_ref[...] = jnp.zeros_like(total_ref)

    forcing = jnp.concatenate([forcing_ref[near, 0] for near in range(NEAR)], axis=0).astype(F32).T
    weighted = perturb_ref[...].astype(F32) * jnp.concatenate([forcing, forcing], axis=0)
    total_ref[...] += jnp.dot(weighted.astype(BF16), lon_block(lon_ref), preferred_element_type=F32)

    @pl.when(step == FAR - 1)
    def _():
        lon_back = total_ref[...].astype(BF16)
        for g in range(8):
            out_ref[:, 256 * g : 256 * g + 256] = lax.dot_general(
                lat_ref[...],
                lon_back[64 * g : 64 * g + 64],
                (((0,), (0,)), ((), ())),
                preferred_element_type=F32,
            ).astype(BF16)


PERTURB_SPEC = pl.BlockSpec((512, 384), lambda far: (0, far))
LON_SPEC = pl.BlockSpec((2, NEAR, 1, 48, 256), lambda far: (0, 0, place(far), 0, 0))
GRID_SPEC = pl.BlockSpec((NEAR, 1, 96, 256), lambda far: (0, place(far), 0, 0))


def whole(*shape):
    return pl.BlockSpec(shape, lambda far: (0,) * len(shape))


def per_device(perturb, control, lat_basis, lon_basis, innovation, weights):
    factor = 1.0 / math.sqrt(63)
    params = pltpu.CompilerParams(vmem_limit_bytes=32 * 2**20)
    core = lax.axis_index("space") % 2

    lon = lax.dynamic_slice_in_dim(lon_basis, core * 48, 48, 0)
    lon = spread(lon, "member", FAR_GROUPS, FAR)
    lon = spread(lon, "member", NEAR_GROUPS, NEAR)
    lon = spread(lon, "space", CORE_GROUPS, 2)

    own = control.reshape(8, 8, 256).transpose(1, 0, 2).reshape(8, 2048)
    full_control = spread(own.astype(BF16), "space", None, 16).reshape(128, 2048)

    perturb = perturb.reshape(512, 3072)
    partial_value = pl.pallas_call(
        forward_kernel,
        grid=(FAR,),
        in_specs=[PERTURB_SPEC, whole(128, 2048), whole(64, 128), LON_SPEC],
        out_specs=GRID_SPEC,
        out_shape=jax.ShapeDtypeStruct((NEAR, FAR, 96, 256), BF16),
        scratch_shapes=[pltpu.VMEM((512, 256), BF16)],
        compiler_params=params,
    )(perturb, full_control, lat_basis, lon)
    parts = lax.all_to_all(partial_value, "member", 0, 0, tiled=True, axis_index_groups=NEAR_GROUPS)
    parts = jnp.sum(parts.astype(F32), axis=0).astype(BF16)
    parts = lax.all_to_all(parts, "member", 0, 0, tiled=True, axis_index_groups=FAR_GROUPS)
    increment, forcing = pl.pallas_call(
        lambda *refs: forcing_kernel(factor, *refs),
        out_shape=(
            jax.ShapeDtypeStruct((256, 96), F32),
            jax.ShapeDtypeStruct((FAR, 96, 256), BF16),
        ),
        compiler_params=params,
    )(parts, innovation.reshape(256, 96), weights.reshape(256, 96))
    forcing = lax.all_to_all(forcing, "member", 0, 0, tiled=True, axis_index_groups=FAR_GROUPS)
    forcing = spread(forcing, "member", NEAR_GROUPS, NEAR)

    projected = pl.pallas_call(
        backward_kernel,
        grid=(FAR,),
        in_specs=[PERTURB_SPEC, GRID_SPEC, whole(64, 128), LON_SPEC],
        out_specs=whole(128, 2048),
        out_shape=jax.ShapeDtypeStruct((128, 2048), BF16),
        scratch_shapes=[pltpu.VMEM((512, 256), F32)],
        compiler_params=params,
    )(perturb, forcing, lat_basis, lon)
    back = lax.all_to_all(projected.reshape(16, 8, 2048), "space", 0, 0, tiled=True)
    back = jnp.sum(back.astype(F32), axis=0).reshape(8, 8, 256).transpose(1, 0, 2)
    gradient = control + factor * back.reshape(control.shape)
    return (increment.reshape(innovation.shape), gradient)


def solution(mesh):
    return jax.shard_map(
        per_device,
        mesh=mesh,
        in_specs=(
            P("member", None, None, "space", None),
            P("member", None, None, "space", None),
            P("space", None),
            P("member", None),
            P(None, None, "space", "member"),
            P(None, None, "space", "member"),
        ),
        out_specs=(P(None, None, "space", "member"), P("member", None, None, "space", None)),
        check_vma=False,
    )
```

```python
import math

import jax
import jax.numpy as jnp
from jax import lax
from jax.experimental import pallas as pl
from jax.experimental.pallas import tpu as pltpu
from jax.sharding import Mesh, PartitionSpec as P

PAIR, RING, NEAR, FAR, PLANE = 2, 16, 2, 8, 32
ORDER = (0, 4, 2, 6, 1, 5, 3, 7)
NEAR_GROUPS = [[NEAR * far + near for near in range(NEAR)] for far in range(FAR)]
FAR_GROUPS = [[NEAR * far + near for far in ORDER] for near in range(NEAR)]
F32, BF16 = jnp.float32, jnp.bfloat16


def place(far):
    return (far % 2) * 4 + (far // 2 % 2) * 2 + far // 4


def columns_kernel(perturb_ref, control_ref, lon_ref, *refs):
    outs, (own_ref, copy_ref, turned_ref) = refs[:PAIR], refs[PAIR:]

    @pl.when(pl.program_id(0) == 0)
    def _():
        copy_ref[...] = lon_ref[...]
        for g in range(8):
            own = control_ref[8 * g : 8 * g + 8, :]
            own = jnp.concatenate([own, own], axis=0).astype(BF16)
            for pair in range(PLANE // 2):
                own_ref[16 * pair : 16 * pair + 16, 256 * g : 256 * g + 256] = own

    turned_ref[...] = perturb_ref[...].astype(F32).T.astype(BF16)
    me = lax.axis_index("pair")
    for other in range(PAIR):
        for z in range(2):
            start = pl.multiple_of(192 * z + 96 * (me ^ other), 96)
            outs[other][96 * z : 96 * z + 96, :] = turned_ref[pl.ds(start, 96), :]


def forward_kernel(own_ref, traded_ref, control_ref, lat_ref, lon_ref, out_ref, part_ref):
    @pl.when(pl.program_id(0) == 0)
    def _():
        for pair in range(PAIR):
            control = control_ref[128 * pair : 128 * pair + 128, :]
            lat_part = jnp.dot(lat_ref[...], control, preferred_element_type=F32).astype(BF16)
            for g in range(8):
                part_ref[pair, 64 * g : 64 * g + 64, :] = lat_part[:, 256 * g : 256 * g + 256]

    me = lax.axis_index("pair")
    total = jnp.zeros((192, 256), F32)
    for other, perturb_ref in enumerate((own_ref, traded_ref)):
        field = lax.dot_general(
            lon_ref[...], part_ref[me ^ other], (((1,), (1,)), ((), ())), preferred_element_type=F32
        )
        terms = perturb_ref[...].astype(F32) * field
        total += terms[:, :256] + terms[:, 256:]
    total = total.astype(BF16)
    for near in range(NEAR):
        out_ref[near, 0] = total[96 * near : 96 * near + 96]


def forcing_kernel(factor, parts_ref, innovation_ref, weights_ref, increment_ref, forcing_ref):
    summed = jnp.sum(parts_ref[...].astype(F32), axis=0) * factor
    increment = summed.T
    increment_ref[...] = increment
    forcing = weights_ref[...].astype(F32) * (increment - innovation_ref[...].astype(F32))
    forcing_ref[...] = forcing.T.astype(BF16)


def backward_kernel(own_ref, traded_ref, forcing_ref, lat_ref, lon_ref, out_ref, total_ref):
    step = pl.program_id(0)

    @pl.when(step == 0)
    def _():
        total_ref[...] = jnp.zeros_like(total_ref)

    forcing = forcing_ref[...].astype(F32)
    forcing = jnp.concatenate([forcing, forcing], axis=1)
    for other, perturb_ref in enumerate((own_ref, traded_ref)):
        weighted = (perturb_ref[...].astype(F32) * forcing).astype(BF16)
        total_ref[other] += lax.dot_general(
            weighted, lon_ref[...], (((0,), (0,)), ((), ())), preferred_element_type=F32
        )

    @pl.when(step == pl.num_programs(0) - 1)
    def _():
        me = lax.axis_index("pair")
        for other in range(PAIR):
            lon_back = total_ref[other].astype(BF16)
            for g in range(8):
                out_ref[me ^ other, :, 256 * g : 256 * g + 256] = lax.dot_general(
                    lat_ref[...],
                    lon_back[64 * g : 64 * g + 64],
                    (((0,), (0,)), ((), ())),
                    preferred_element_type=F32,
                ).astype(BF16)


def whole(*shape):
    return pl.BlockSpec(shape, lambda step: (0,) * len(shape))


def rows_of(rows, width):
    return pl.BlockSpec((rows, width), lambda step: (step, 0))


def shape_of(shape, dtype=BF16):
    return jax.ShapeDtypeStruct(shape, dtype)


def per_device(perturb, control, lat_basis, lon_basis, innovation, weights):
    factor = 1.0 / math.sqrt(63)
    params = pltpu.CompilerParams(vmem_limit_bytes=40 * 2**20)

    own, other, own_control, lon = pl.pallas_call(
        columns_kernel,
        grid=(8,),
        in_specs=[pl.BlockSpec((512, 384), lambda step: (0, step)), whole(64, 256), whole(96, 256)],
        out_specs=[rows_of(192, 512)] * PAIR + [whole(8 * PLANE, 2048), whole(96, 256)],
        out_shape=[shape_of((1536, 512))] * PAIR + [shape_of((8 * PLANE, 2048)), shape_of((96, 256))],
        scratch_shapes=[pltpu.VMEM((384, 512), BF16)],
        compiler_params=params,
    )(perturb.reshape(512, 3072), control.reshape(64, 256), lon_basis)
    traded = lax.ppermute(other, "pair", [(0, 1), (1, 0)])
    full_control = lax.all_to_all(own_control, ("pair", "space"), 0, 0, tiled=True)
    lon = lax.all_gather(lon, "z", axis=0, tiled=True)

    parts = pl.pallas_call(
        forward_kernel,
        grid=(8,),
        in_specs=[rows_of(192, 512)] * PAIR + [whole(256, 2048), whole(64, 128), rows_of(192, 256)],
        out_specs=pl.BlockSpec((NEAR, 1, 96, 256), lambda step: (0, place(step), 0, 0)),
        out_shape=shape_of((NEAR, FAR, 96, 256)),
        scratch_shapes=[pltpu.VMEM((PAIR, 512, 256), BF16)],
        compiler_params=params,
    )(own, traded, full_control, lat_basis, lon)
    parts = lax.all_to_all(parts, "z", 0, 0, tiled=True, axis_index_groups=NEAR_GROUPS)
    parts = jnp.sum(parts.astype(F32), axis=0).astype(BF16)
    parts = lax.all_to_all(parts, "z", 0, 0, tiled=True, axis_index_groups=FAR_GROUPS)
    increment, forcing = pl.pallas_call(
        lambda *refs: forcing_kernel(factor, *refs),
        out_shape=(shape_of((256, 96), F32), shape_of((96, 256))),
        compiler_params=params,
    )(parts, innovation.reshape(256, 96), weights.reshape(256, 96))
    forcing = lax.all_gather(forcing, "z", axis=0, tiled=True)

    projected = pl.pallas_call(
        backward_kernel,
        grid=(6,),
        in_specs=[rows_of(256, 512)] * PAIR + [rows_of(256, 256), whole(64, 128), rows_of(256, 256)],
        out_specs=whole(PAIR, 128, 2048),
        out_shape=shape_of((PAIR, 128, 2048)),
        scratch_shapes=[pltpu.VMEM((PAIR, 512, 256), F32)],
        compiler_params=params,
    )(own, traded, forcing, lat_basis, lon)
    back = lax.all_to_all(projected.reshape(8 * PLANE, 2048), ("pair", "space"), 0, 0, tiled=True)
    back = jnp.sum(back.astype(F32).reshape(PLANE, 8, 2048), axis=0)
    back = back.reshape(8, 8, 256).transpose(1, 0, 2)
    gradient = control + factor * back.reshape(control.shape)
    return (increment.reshape(innovation.shape), gradient)


def solution(mesh):
    members = ("z", "pair")
    devices = mesh.devices.reshape(RING, PAIR, mesh.shape["space"])
    return jax.shard_map(
        per_device,
        mesh=Mesh(devices, (*members, "space")),
        in_specs=(
            P(members, None, None, "space", None),
            P(members, None, None, "space", None),
            P("space", None),
            P(members, None),
            P(None, None, "space", members),
            P(None, None, "space", members),
        ),
        out_specs=(P(None, None, "space", members), P(members, None, None, "space", None)),
        check_vma=False,
    )
```

```python
import math

import jax
import jax.numpy as jnp
from jax import lax
from jax.experimental import pallas as pl
from jax.experimental.pallas import tpu as pltpu
from jax.sharding import Mesh, PartitionSpec as P

PAIR, RING, CHIPS, CORES, NEAR, FAR = 2, 16, 8, 2, 2, 8
ORDER = (0, 4, 2, 6, 1, 5, 3, 7)
NEAR_GROUPS = [[NEAR * far + near for near in range(NEAR)] for far in range(FAR)]
FAR_GROUPS = [[NEAR * far + near for far in ORDER] for near in range(NEAR)]
SWAP = [(0, 1), (1, 0)]
F32, BF16 = jnp.float32, jnp.bfloat16


def place(far):
    return ((far & 1) << 2) | (far & 2) | (far >> 2)


def half_basis(lat_ref, core):
    held = lax.broadcasted_iota(jnp.int32, (128, 64), 0)
    wanted = lax.broadcasted_iota(jnp.int32, (128, 64), 1)
    wanted = ((wanted >> 3) << 4) + (wanted & 7) + 8 * core
    pick = jnp.where(held == wanted, 1.0, 0.0).astype(BF16)
    return jnp.dot(lat_ref[...], pick, preferred_element_type=F32).astype(BF16)


def columns_kernel(perturb_ref, lon_ref, *refs):
    outs, (copy_ref, turned_ref) = refs[:PAIR], refs[PAIR:]
    copy_ref[...] = lon_ref[...]
    turned_ref[...] = perturb_ref[...].astype(F32).T.astype(BF16)
    me = lax.axis_index("pair")
    for other in range(PAIR):
        for z in range(RING):
            start = pl.multiple_of(192 * z + 96 * (me ^ other), 96)
            outs[other][0, 96 * z : 96 * z + 96, :] = turned_ref[pl.ds(start, 96), :]


def forward_kernel(own_ref, traded_ref, control_ref, lat_ref, lon_ref, out_ref, part_ref):
    step = pl.program_id(0)

    @pl.when(step == 0)
    def _():
        for pair in range(PAIR):
            control = control_ref[128 * pair : 128 * pair + 128, :]
            lat_part = jnp.dot(lat_ref[...], control, preferred_element_type=F32).astype(BF16)
            for g in range(8):
                part_ref[pair, 64 * g : 64 * g + 64, :] = lat_part[:, 256 * g : 256 * g + 256]

    me = lax.axis_index("pair")
    halves = [jnp.zeros((384, 128), F32), jnp.zeros((384, 128), F32)]
    for other, perturb_ref in enumerate((own_ref, traded_ref)):
        field = lax.dot_general(
            lon_ref[...], part_ref[me ^ other], (((1,), (1,)), ((), ())), preferred_element_type=F32
        )
        for block in range(4):
            halves[block % 2] += perturb_ref[block].astype(F32) * field[:, 128 * block : 128 * block + 128]
    for half in range(2):
        total = halves[half].astype(BF16)
        for z in range(4):
            far = 2 * step + z // 2
            out_ref[z % 2, place(far), :, 128 * half : 128 * half + 128] = total[96 * z : 96 * z + 96]


def forcing_kernel(factor, parts_ref, innovation_ref, weights_ref, increment_ref, forcing_ref):
    summed = jnp.sum(parts_ref[...].astype(F32), axis=0) * factor
    increment = summed.T
    increment_ref[...] = increment
    forcing = weights_ref[...].astype(F32) * (increment - innovation_ref[...].astype(F32))
    forcing_ref[...] = forcing.T.astype(BF16)


def backward_kernel(own_ref, traded_ref, forcing_ref, lat_ref, lon_ref, keep_ref, give_ref, total_ref):
    step = pl.program_id(0)

    @pl.when(step == 0)
    def _():
        total_ref[...] = jnp.zeros_like(total_ref)

    forcing = forcing_ref[...].astype(F32)
    for other, perturb_ref in enumerate((own_ref, traded_ref)):
        for block in range(4):
            half = 128 * (block % 2)
            weighted = (perturb_ref[block].astype(F32) * forcing[:, half : half + 128]).astype(BF16)
            total_ref[other, 128 * block : 128 * block + 128, :] += lax.dot_general(
                weighted, lon_ref[...], (((0,), (0,)), ((), ())), preferred_element_type=F32
            )

    @pl.when(step == pl.num_programs(0) - 1)
    def _():
        me, core = lax.axis_index("pair"), lax.axis_index("core")
        lat_mine, lat_swapped = half_basis(lat_ref, core), half_basis(lat_ref, 1 - core)
        for other in range(PAIR):
            rows = pl.ds(pl.multiple_of(64 * (me ^ other), 64), 64)
            lon_back = total_ref[other].astype(BF16)
            for g in range(8):
                part = lon_back[64 * g : 64 * g + 64]
                for lat, out_ref in ((lat_mine, keep_ref), (lat_swapped, give_ref)):
                    out_ref[rows, 256 * g : 256 * g + 256] = lax.dot_general(
                        lat, part, (((0,), (0,)), ((), ())), preferred_element_type=F32
                    ).astype(out_ref.dtype)


def add_kernel(keep_ref, got_ref, out_ref):
    out_ref[...] = (keep_ref[...] + got_ref[...].astype(F32)).astype(BF16)


def whole(*shape):
    return pl.BlockSpec(shape, lambda step: (0,) * len(shape))


def rows_of(*shape):
    return pl.BlockSpec(shape, lambda step: (0,) * (len(shape) - 2) + (step, 0))


def shape_of(shape, dtype=BF16):
    return jax.ShapeDtypeStruct(shape, dtype)


def per_device(perturb, control, lat_basis, lon_basis, innovation, weights):
    factor = 1.0 / math.sqrt(63)
    params = pltpu.CompilerParams(vmem_limit_bytes=40 * 2**20)

    own_control = control.reshape(8, 8, 256).transpose(1, 0, 2).reshape(8, 2048).astype(BF16)
    own_control = jnp.broadcast_to(own_control, (PAIR * CHIPS * CORES, 8, 2048)).reshape(256, 2048)
    own, other, lon = pl.pallas_call(
        columns_kernel,
        grid=(4,),
        in_specs=[rows_of(128, 3072), whole(96, 256)],
        out_specs=[pl.BlockSpec((1, 1536, 128), lambda step: (step, 0, 0))] * PAIR + [whole(96, 256)],
        out_shape=[shape_of((4, 1536, 128))] * PAIR + [shape_of((96, 256))],
        scratch_shapes=[pltpu.VMEM((3072, 128), BF16)],
        compiler_params=pltpu.CompilerParams(vmem_limit_bytes=60 * 2**20),
    )(perturb.reshape(512, 3072), lon_basis)
    traded = lax.ppermute(other, "pair", SWAP)
    lon = lax.all_gather(lon, "z", axis=0, tiled=True)
    full_control = lax.all_to_all(own_control, ("pair", "chip", "core"), 0, 0, tiled=True)

    parts = pl.pallas_call(
        forward_kernel,
        grid=(4,),
        in_specs=[rows_of(4, 384, 128)] * PAIR
        + [whole(256, 2048), whole(64, 128), rows_of(384, 256)],
        out_specs=whole(NEAR, FAR, 96, 256),
        out_shape=shape_of((NEAR, FAR, 96, 256)),
        scratch_shapes=[pltpu.VMEM((PAIR, 512, 256), BF16)],
        compiler_params=params,
    )(own, traded, full_control, lat_basis, lon)
    parts = lax.all_to_all(parts, "z", 0, 0, tiled=True, axis_index_groups=NEAR_GROUPS)
    parts = jnp.sum(parts.astype(F32), axis=0).astype(BF16)
    parts = lax.all_to_all(parts, "z", 0, 0, tiled=True, axis_index_groups=FAR_GROUPS)
    increment, forcing = pl.pallas_call(
        lambda *refs: forcing_kernel(factor, *refs),
        out_shape=(shape_of((256, 96), F32), shape_of((96, 256))),
        compiler_params=params,
    )(parts, innovation.reshape(256, 96), weights.reshape(256, 96))
    forcing = lax.all_gather(forcing, "z", axis=0, tiled=True)

    keep, give = pl.pallas_call(
        backward_kernel,
        grid=(3,),
        in_specs=[rows_of(4, 512, 128)] * PAIR + [rows_of(512, 256), whole(64, 128), rows_of(512, 256)],
        out_specs=[whole(128, 2048)] * 2,
        out_shape=[shape_of((128, 2048), F32), shape_of((128, 2048))],
        scratch_shapes=[pltpu.VMEM((PAIR, 512, 256), F32)],
        compiler_params=params,
    )(own, traded, forcing, lat_basis, lon)
    got = lax.ppermute(give, "core", SWAP)
    back = pl.pallas_call(add_kernel, out_shape=shape_of((128, 2048)), compiler_params=params)(keep, got)
    back = lax.all_to_all(back, ("pair", "chip"), 0, 0, tiled=True)
    back = jnp.sum(back.astype(F32).reshape(PAIR * CHIPS, 8, 2048), axis=0)
    back = back.reshape(8, 8, 256).transpose(1, 0, 2)
    gradient = control + factor * back.reshape(control.shape)
    return (increment.reshape(innovation.shape), gradient)


def solution(mesh):
    members, space = ("z", "pair"), ("chip", "core")
    devices = mesh.devices.reshape(RING, PAIR, CHIPS, CORES)
    return jax.shard_map(
        per_device,
        mesh=Mesh(devices, (*members, *space)),
        in_specs=(
            P(members, None, None, space, None),
            P(members, None, None, space, None),
            P(space, None),
            P(members, None),
            P(None, None, space, members),
            P(None, None, space, members),
        ),
        out_specs=(P(None, None, space, members), P(members, None, None, space, None)),
        check_vma=False,
    )
```

```python
import math

import jax
import jax.numpy as jnp
from jax import lax
from jax.experimental import pallas as pl
from jax.experimental.pallas import tpu as pltpu
from jax.sharding import Mesh, PartitionSpec as P

PAIR, RING, CHIPS, CORES, FAR = 2, 16, 8, 2, 8
ORDER = (0, 4, 2, 6, 1, 5, 3, 7)
FAR_GROUPS = [[2 * far + parity for far in ORDER] for parity in range(2)]
SWAP = [(0, 1), (1, 0)]
F32, BF16 = jnp.float32, jnp.bfloat16


def place(far):
    return ((far & 1) << 2) | (far & 2) | (far >> 2)


def z_parity():
    return lax.axis_index("z") & 1


def half_basis(lat_ref, core):
    held = lax.broadcasted_iota(jnp.int32, (128, 64), 0)
    wanted = lax.broadcasted_iota(jnp.int32, (128, 64), 1)
    wanted = ((wanted >> 3) << 4) + (wanted & 7) + 8 * core
    pick = jnp.where(held == wanted, 1.0, 0.0).astype(BF16)
    return jnp.dot(lat_ref[...], pick, preferred_element_type=F32).astype(BF16)


def columns(perturb_ref, turned_ref, outs):
    turned_ref[...] = perturb_ref[...].astype(F32).T.astype(BF16)
    parity = z_parity()
    for pair, out_ref in outs:
        for half in range(2):
            for far in range(FAR):
                row = 96 * (FAR * half + far)
                start = pl.multiple_of(384 * far + 192 * (1 - half ^ parity) + 96 * pair, 96)
                out_ref[0, row : row + 96, :] = turned_ref[pl.ds(start, 96), :]


def first_kernel(perturb_ref, first_ref, turned_ref):
    columns(perturb_ref, turned_ref, [(1 - lax.axis_index("pair"), first_ref)])


def columns_kernel(perturb_ref, lon_ref, before_ref, own_ref, second_ref, copy_ref, turned_ref):
    copy_ref[...] = lon_ref[...]
    me = lax.axis_index("pair")

    @pl.when(pl.program_id(0) < 2)
    def _():
        columns(perturb_ref, turned_ref, [(1 - me, second_ref), (me, own_ref)])

    @pl.when(pl.program_id(0) >= 2)
    def _():
        columns(perturb_ref, turned_ref, [(me, own_ref)])


def perturb_block(own_ref, first_ref, second_ref, other, block):
    if other == 0:
        return own_ref[block].astype(F32)
    return (first_ref, second_ref)[block // 2][block % 2].astype(F32)


def terms(own_ref, first_ref, second_ref, part_ref, lon):
    me = lax.axis_index("pair")
    halves = [jnp.zeros((192, 128), F32), jnp.zeros((192, 128), F32)]
    for other in range(PAIR):
        field = lax.dot_general(
            lon, part_ref[me ^ other], (((1,), (1,)), ((), ())), preferred_element_type=F32
        )
        for block in range(4):
            perturb = perturb_block(own_ref, first_ref, second_ref, other, block)
            halves[block % 2] += perturb * field[:, 128 * block : 128 * block + 128]
    return halves


def store_terms(halves, out_ref):
    step = pl.program_id(0)
    for half in range(2):
        total = halves[half].astype(out_ref.dtype)
        for i in range(2):
            out_ref[place(2 * step + i), :, 128 * half : 128 * half + 128] = total[96 * i : 96 * i + 96]


def forward_kernel(own_ref, first_ref, second_ref, control_ref, lat_ref, lon_ref, out_ref, part_ref):
    @pl.when(pl.program_id(0) == 0)
    def _():
        for pair in range(PAIR):
            control = control_ref[128 * pair : 128 * pair + 128, :]
            lat_part = jnp.dot(lat_ref[...], control, preferred_element_type=F32).astype(BF16)
            for g in range(8):
                part_ref[pair, 64 * g : 64 * g + 64, :] = lat_part[:, 256 * g : 256 * g + 256]

    lon = lon_ref[:, 1 - z_parity()].reshape(192, 256)
    store_terms(terms(own_ref, first_ref, second_ref, part_ref, lon), out_ref)


def forward_own_kernel(own_ref, first_ref, second_ref, part_ref, lon_ref, out_ref):
    lon = lon_ref[:, z_parity()].reshape(192, 256)
    store_terms(terms(own_ref, first_ref, second_ref, part_ref, lon), out_ref)


def forcing_kernel(factor, parts_ref, innovation_ref, weights_ref, increment_ref, forcing_ref):
    summed = jnp.sum(parts_ref[...].astype(F32), axis=0) * factor
    increment = summed.T
    increment_ref[...] = increment
    forcing = weights_ref[...].astype(F32) * (increment - innovation_ref[...].astype(F32))
    forcing_ref[...] = forcing.T.astype(BF16)


def backward_kernel(own_ref, first_ref, second_ref, forcing_ref, lat_ref, lon_ref, keep_ref, give_ref, total_ref):
    step = pl.program_id(0)

    @pl.when(step == 0)
    def _():
        total_ref[...] = jnp.zeros_like(total_ref)

    half = jnp.where(step < 2, 1, 0) ^ z_parity()
    lon = lon_ref[:, half].reshape(384, 256)
    forcing = forcing_ref[:, half].reshape(384, 256).astype(F32)
    for other in range(PAIR):
        for block in range(4):
            lanes = slice(128 * (block % 2), 128 * (block % 2) + 128)
            perturb = perturb_block(own_ref, first_ref, second_ref, other, block)
            weighted = (perturb * forcing[:, lanes]).astype(BF16)
            total_ref[other, 128 * block : 128 * block + 128, :] += lax.dot_general(
                weighted, lon, (((0,), (0,)), ((), ())), preferred_element_type=F32
            )

    @pl.when(step == pl.num_programs(0) - 1)
    def _():
        me, core = lax.axis_index("pair"), lax.axis_index("core")
        lat_mine, lat_swapped = half_basis(lat_ref, core), half_basis(lat_ref, 1 - core)
        for other in range(PAIR):
            rows = pl.ds(pl.multiple_of(64 * (me ^ other), 64), 64)
            lon_back = total_ref[other].astype(BF16)
            for g in range(8):
                part = lon_back[64 * g : 64 * g + 64]
                for lat, out_ref in ((lat_mine, keep_ref), (lat_swapped, give_ref)):
                    out_ref[rows, 256 * g : 256 * g + 256] = lax.dot_general(
                        lat, part, (((0,), (0,)), ((), ())), preferred_element_type=F32
                    ).astype(out_ref.dtype)


def add_kernel(keep_ref, got_ref, out_ref):
    out_ref[...] = (keep_ref[...] + got_ref[...].astype(F32)).astype(BF16)


def gradient_kernel(factor, back_ref, control_ref, out_ref):
    back = jnp.sum(back_ref[...].astype(F32).reshape(PAIR * CHIPS, 8, 2048), axis=0) * factor
    for g in range(8):
        rows = slice(8 * g, 8 * g + 8)
        out_ref[rows, :] = control_ref[rows, :] + back[:, 256 * g : 256 * g + 256]


def whole(*shape):
    return pl.BlockSpec(shape, lambda step: (0,) * len(shape))


def rows_of(*shape):
    return pl.BlockSpec(shape, lambda step: (0,) * (len(shape) - 2) + (step, 0))


def shape_of(shape, dtype=BF16):
    return jax.ShapeDtypeStruct(shape, dtype)


def per_device(perturb, control, lat_basis, lon_basis, innovation, weights):
    factor = 1.0 / math.sqrt(63)
    params = pltpu.CompilerParams(vmem_limit_bytes=20 * 2**20)

    own_control = control.reshape(8, 8, 256).transpose(1, 0, 2).reshape(8, 2048).astype(BF16)
    own_control = jnp.broadcast_to(own_control, (PAIR * CHIPS * CORES, 8, 2048)).reshape(256, 2048)
    large = pltpu.CompilerParams(vmem_limit_bytes=60 * 2**20)
    perturb = perturb.reshape(512, 3072)

    def block_of(index):
        return pl.BlockSpec((1, 1536, 128), lambda step: (index(step), 0, 0))

    first = pl.pallas_call(
        first_kernel,
        grid=(2,),
        in_specs=[rows_of(128, 3072)],
        out_specs=block_of(lambda step: step),
        out_shape=shape_of((2, 1536, 128)),
        scratch_shapes=[pltpu.VMEM((3072, 128), BF16)],
        compiler_params=large,
    )(perturb)
    own, second, lon = pl.pallas_call(
        columns_kernel,
        grid=(4,),
        in_specs=[
            pl.BlockSpec((128, 3072), lambda step: (step ^ 2, 0)),
            whole(96, 256),
            pl.BlockSpec(memory_space=pl.ANY),
        ],
        out_specs=[
            block_of(lambda step: step ^ 2),
            block_of(lambda step: jnp.minimum(step, 1)),
            whole(96, 256),
        ],
        out_shape=[shape_of((4, 1536, 128)), shape_of((2, 1536, 128)), shape_of((96, 256))],
        scratch_shapes=[pltpu.VMEM((3072, 128), BF16)],
        compiler_params=large,
    )(perturb, lon_basis, first)
    first = lax.ppermute(first, "pair", SWAP)
    second = lax.ppermute(second, "pair", SWAP)
    lon = lax.all_gather(lon, "z", axis=0, tiled=True)
    full_control = lax.all_to_all(own_control, ("pair", "chip", "core"), 0, 0, tiled=True)

    lon = lon.reshape(FAR, 2, 96, 256)

    def later(*shape):
        return pl.BlockSpec(shape, lambda step: (0, step + 4, 0))

    lon_spec = pl.BlockSpec((2, 2, 96, 256), lambda step: (step, 0, 0, 0))
    give, lat_part = pl.pallas_call(
        forward_kernel,
        grid=(4,),
        in_specs=[rows_of(4, 192, 128), rows_of(2, 192, 128), rows_of(2, 192, 128)]
        + [whole(256, 2048), whole(64, 128), lon_spec],
        out_specs=[whole(FAR, 96, 256), whole(PAIR, 512, 256)],
        out_shape=[shape_of((FAR, 96, 256)), shape_of((PAIR, 512, 256))],
        compiler_params=params,
    )(own, first, second, full_control, lat_basis, lon)
    got = lax.ppermute(give, "z", [(z, z ^ 1) for z in range(RING)])
    keep = pl.pallas_call(
        forward_own_kernel,
        grid=(4,),
        in_specs=[later(4, 192, 128), later(2, 192, 128), later(2, 192, 128)]
        + [whole(PAIR, 512, 256), lon_spec],
        out_specs=whole(FAR, 96, 256),
        out_shape=shape_of((FAR, 96, 256), F32),
        compiler_params=params,
    )(own, first, second, lat_part, lon)
    parts = pl.pallas_call(add_kernel, out_shape=shape_of((FAR, 96, 256)), compiler_params=params)(keep, got)
    parts = lax.all_to_all(parts, "z", 0, 0, tiled=True, axis_index_groups=FAR_GROUPS)
    increment, forcing = pl.pallas_call(
        lambda *refs: forcing_kernel(factor, *refs),
        out_shape=(shape_of((256, 96), F32), shape_of((96, 256))),
        compiler_params=params,
    )(parts, innovation.reshape(256, 96), weights.reshape(256, 96))
    forcing = lax.all_gather(forcing, "z", axis=0, tiled=True).reshape(FAR, 2, 96, 256)
    half_spec = pl.BlockSpec((4, 2, 96, 256), lambda step: (lax.rem(step, 2), 0, 0, 0))

    keep, give = pl.pallas_call(
        backward_kernel,
        grid=(4,),
        in_specs=[rows_of(4, 384, 128), rows_of(2, 384, 128), rows_of(2, 384, 128)]
        + [half_spec, whole(64, 128), half_spec],
        out_specs=[whole(128, 2048)] * 2,
        out_shape=[shape_of((128, 2048), F32), shape_of((128, 2048))],
        scratch_shapes=[pltpu.VMEM((PAIR, 512, 256), F32)],
        compiler_params=params,
    )(own, first, second, forcing, lat_basis, lon)
    got = lax.ppermute(give, "core", SWAP)
    back = pl.pallas_call(add_kernel, out_shape=shape_of((128, 2048)), compiler_params=params)(keep, got)
    back = lax.all_to_all(back, ("pair", "chip"), 0, 0, tiled=True)
    gradient = pl.pallas_call(
        lambda *refs: gradient_kernel(factor, *refs),
        out_shape=shape_of((64, 256), F32),
        compiler_params=params,
    )(back, control.reshape(64, 256))
    return (increment.reshape(innovation.shape), gradient.reshape(control.shape))


def solution(mesh):
    members, space = ("z", "pair"), ("chip", "core")
    devices = mesh.devices.reshape(RING, PAIR, CHIPS, CORES)
    return jax.shard_map(
        per_device,
        mesh=Mesh(devices, (*members, *space)),
        in_specs=(
            P(members, None, None, space, None),
            P(members, None, None, space, None),
            P(space, None),
            P(members, None),
            P(None, None, space, members),
            P(None, None, space, members),
        ),
        out_specs=(P(None, None, space, members), P(members, None, None, space, None)),
        check_vma=False,
    )
```

```python
import math

import jax
import jax.numpy as jnp
from jax import lax
from jax.experimental import pallas as pl
from jax.experimental.pallas import tpu as pltpu
from jax.sharding import Mesh, PartitionSpec as P

PAIR, RING, CHIPS, CORES, FAR = 2, 16, 8, 2, 8
ORDER = (0, 4, 2, 6, 1, 5, 3, 7)
FAR_GROUPS = [[2 * far + parity for far in ORDER] for parity in range(2)]
SWAP = [(0, 1), (1, 0)]
BACKWARD = [[RING - 1 - z for z in range(RING)]]
F32, BF16 = jnp.float32, jnp.bfloat16


def place(far):
    return ((far & 1) << 2) | (far & 2) | (far >> 2)


def z_parity():
    return lax.axis_index("z") & 1


def half_basis(lat_ref, core):
    held = lax.broadcasted_iota(jnp.int32, (128, 64), 0)
    wanted = lax.broadcasted_iota(jnp.int32, (128, 64), 1)
    wanted = ((wanted >> 3) << 4) + (wanted & 7) + 8 * core
    pick = jnp.where(held == wanted, 1.0, 0.0).astype(BF16)
    return jnp.dot(lat_ref[...], pick, preferred_element_type=F32).astype(BF16)


def columns(perturb_ref, turned_ref, outs):
    turned_ref[...] = perturb_ref[...].astype(F32).T.astype(BF16)
    parity = z_parity()
    for pair, out_ref in outs:
        for half in range(2):
            for far in range(FAR):
                row = 96 * (FAR * half + far)
                start = pl.multiple_of(384 * far + 192 * (1 - half ^ parity) + 96 * pair, 96)
                out_ref[0, row : row + 96, :] = turned_ref[pl.ds(start, 96), :]


def first_kernel(perturb_ref, first_ref, turned_ref):
    columns(perturb_ref, turned_ref, [(1 - lax.axis_index("pair"), first_ref)])


def columns_kernel(perturb_ref, lon_ref, before_ref, own_ref, second_ref, copy_ref, turned_ref):
    copy_ref[...] = lon_ref[...]
    me = lax.axis_index("pair")

    @pl.when(pl.program_id(0) < 2)
    def _():
        columns(perturb_ref, turned_ref, [(1 - me, second_ref), (me, own_ref)])

    @pl.when(pl.program_id(0) >= 2)
    def _():
        columns(perturb_ref, turned_ref, [(me, own_ref)])


def perturb_block(own_ref, first_ref, second_ref, other, block):
    if other == 0:
        return own_ref[block].astype(F32)
    return (first_ref, second_ref)[block // 2][block % 2].astype(F32)


def terms(own_ref, first_ref, second_ref, part_ref, lon):
    me = lax.axis_index("pair")
    halves = [jnp.zeros((192, 128), F32), jnp.zeros((192, 128), F32)]
    for other in range(PAIR):
        field = lax.dot_general(
            lon, part_ref[me ^ other], (((1,), (1,)), ((), ())), preferred_element_type=F32
        )
        for block in range(4):
            perturb = perturb_block(own_ref, first_ref, second_ref, other, block)
            halves[block % 2] += perturb * field[:, 128 * block : 128 * block + 128]
    return halves


def store_terms(halves, out_ref):
    step = pl.program_id(0)
    for half in range(2):
        total = halves[half].astype(out_ref.dtype)
        for i in range(2):
            out_ref[place(2 * step + i), :, 128 * half : 128 * half + 128] = total[96 * i : 96 * i + 96]


def forward_kernel(own_ref, first_ref, second_ref, control_ref, lat_ref, lon_ref, out_ref, part_ref):
    @pl.when(pl.program_id(0) == 0)
    def _():
        for pair in range(PAIR):
            control = control_ref[128 * pair : 128 * pair + 128, :]
            lat_part = jnp.dot(lat_ref[...], control, preferred_element_type=F32).astype(BF16)
            for g in range(8):
                part_ref[pair, 64 * g : 64 * g + 64, :] = lat_part[:, 256 * g : 256 * g + 256]

    lon = lon_ref[:, 1 - z_parity()].reshape(192, 256)
    store_terms(terms(own_ref, first_ref, second_ref, part_ref, lon), out_ref)


def forward_own_kernel(own_ref, first_ref, second_ref, part_ref, lon_ref, out_ref):
    lon = lon_ref[:, z_parity()].reshape(192, 256)
    store_terms(terms(own_ref, first_ref, second_ref, part_ref, lon), out_ref)


def forcing_kernel(factor, parts_ref, innovation_ref, weights_ref, increment_ref, forcing_ref):
    summed = jnp.sum(parts_ref[...].astype(F32), axis=0) * factor
    increment = summed.T
    increment_ref[...] = increment
    forcing = weights_ref[...].astype(F32) * (increment - innovation_ref[...].astype(F32))
    forcing_ref[...] = forcing.T.astype(BF16)


def backward_kernel(own_ref, first_ref, second_ref, forcing_ref, lat_ref, lon_ref, keep_ref, give_ref, total_ref):
    step = pl.program_id(0)

    @pl.when(step == 0)
    def _():
        total_ref[...] = jnp.zeros_like(total_ref)

    half = jnp.where(step < 2, 1, 0) ^ z_parity()
    lon = lon_ref[:, half].reshape(384, 256)
    forcing = jnp.concatenate([forcing_ref[3 - far, 1 - half] for far in range(4)], axis=0).astype(F32)
    for other in range(PAIR):
        for block in range(4):
            lanes = slice(128 * (block % 2), 128 * (block % 2) + 128)
            perturb = perturb_block(own_ref, first_ref, second_ref, other, block)
            weighted = (perturb * forcing[:, lanes]).astype(BF16)
            total_ref[other, 128 * block : 128 * block + 128, :] += lax.dot_general(
                weighted, lon, (((0,), (0,)), ((), ())), preferred_element_type=F32
            )

    @pl.when(step == pl.num_programs(0) - 1)
    def _():
        me, core = lax.axis_index("pair"), lax.axis_index("core")
        lat_mine, lat_swapped = half_basis(lat_ref, core), half_basis(lat_ref, 1 - core)
        for other in range(PAIR):
            rows = pl.ds(pl.multiple_of(64 * (me ^ other), 64), 64)
            lon_back = total_ref[other].astype(BF16)
            for g in range(8):
                part = lon_back[64 * g : 64 * g + 64]
                for lat, out_ref in ((lat_mine, keep_ref), (lat_swapped, give_ref)):
                    out_ref[rows, 256 * g : 256 * g + 256] = lax.dot_general(
                        lat, part, (((0,), (0,)), ((), ())), preferred_element_type=F32
                    ).astype(out_ref.dtype)


def add_kernel(keep_ref, got_ref, out_ref):
    out_ref[...] = (keep_ref[...] + got_ref[...].astype(F32)).astype(BF16)


def gradient_kernel(factor, back_ref, control_ref, out_ref):
    back = jnp.sum(back_ref[...].astype(F32).reshape(PAIR * CHIPS, 8, 2048), axis=0) * factor
    for g in range(8):
        rows = slice(8 * g, 8 * g + 8)
        out_ref[rows, :] = control_ref[rows, :] + back[:, 256 * g : 256 * g + 256]


def whole(*shape):
    return pl.BlockSpec(shape, lambda step: (0,) * len(shape))


def rows_of(*shape):
    return pl.BlockSpec(shape, lambda step: (0,) * (len(shape) - 2) + (step, 0))


def shape_of(shape, dtype=BF16):
    return jax.ShapeDtypeStruct(shape, dtype)


def per_device(perturb, control, lat_basis, lon_basis, innovation, weights):
    factor = 1.0 / math.sqrt(63)
    params = pltpu.CompilerParams(vmem_limit_bytes=20 * 2**20)

    own_control = control.reshape(8, 8, 256).transpose(1, 0, 2).reshape(8, 2048).astype(BF16)
    own_control = jnp.broadcast_to(own_control, (PAIR * CHIPS * CORES, 8, 2048)).reshape(256, 2048)
    large = pltpu.CompilerParams(vmem_limit_bytes=60 * 2**20)
    perturb = perturb.reshape(512, 3072)

    def block_of(index):
        return pl.BlockSpec((1, 1536, 128), lambda step: (index(step), 0, 0))

    first = pl.pallas_call(
        first_kernel,
        grid=(2,),
        in_specs=[rows_of(128, 3072)],
        out_specs=block_of(lambda step: step),
        out_shape=shape_of((2, 1536, 128)),
        scratch_shapes=[pltpu.VMEM((3072, 128), BF16)],
        compiler_params=large,
    )(perturb)
    own, second, lon = pl.pallas_call(
        columns_kernel,
        grid=(4,),
        in_specs=[
            pl.BlockSpec((128, 3072), lambda step: (step ^ 2, 0)),
            whole(96, 256),
            pl.BlockSpec(memory_space=pl.ANY),
        ],
        out_specs=[
            block_of(lambda step: step ^ 2),
            block_of(lambda step: jnp.minimum(step, 1)),
            whole(96, 256),
        ],
        out_shape=[shape_of((4, 1536, 128)), shape_of((2, 1536, 128)), shape_of((96, 256))],
        scratch_shapes=[pltpu.VMEM((3072, 128), BF16)],
        compiler_params=large,
    )(perturb, lon_basis, first)
    first = lax.ppermute(first, "pair", SWAP)
    second = lax.ppermute(second, "pair", SWAP)
    lon = lax.all_gather(lon, "z", axis=0, tiled=True)
    full_control = lax.all_to_all(own_control, ("pair", "chip", "core"), 0, 0, tiled=True)

    lon = lon.reshape(FAR, 2, 96, 256)

    def later(*shape):
        return pl.BlockSpec(shape, lambda step: (0, step + 4, 0))

    lon_spec = pl.BlockSpec((2, 2, 96, 256), lambda step: (step, 0, 0, 0))
    give, lat_part = pl.pallas_call(
        forward_kernel,
        grid=(4,),
        in_specs=[rows_of(4, 192, 128), rows_of(2, 192, 128), rows_of(2, 192, 128)]
        + [whole(256, 2048), whole(64, 128), lon_spec],
        out_specs=[whole(FAR, 96, 256), whole(PAIR, 512, 256)],
        out_shape=[shape_of((FAR, 96, 256)), shape_of((PAIR, 512, 256))],
        compiler_params=params,
    )(own, first, second, full_control, lat_basis, lon)
    got = lax.ppermute(give, "z", [(z, z ^ 1) for z in range(RING)])
    keep = pl.pallas_call(
        forward_own_kernel,
        grid=(4,),
        in_specs=[later(4, 192, 128), later(2, 192, 128), later(2, 192, 128)]
        + [whole(PAIR, 512, 256), lon_spec],
        out_specs=whole(FAR, 96, 256),
        out_shape=shape_of((FAR, 96, 256), F32),
        compiler_params=params,
    )(own, first, second, lat_part, lon)
    parts = pl.pallas_call(add_kernel, out_shape=shape_of((FAR, 96, 256)), compiler_params=params)(keep, got)
    parts = lax.all_to_all(parts, "z", 0, 0, tiled=True, axis_index_groups=FAR_GROUPS)
    increment, forcing = pl.pallas_call(
        lambda *refs: forcing_kernel(factor, *refs),
        out_shape=(shape_of((256, 96), F32), shape_of((96, 256))),
        compiler_params=params,
    )(parts, innovation.reshape(256, 96), weights.reshape(256, 96))
    forcing = lax.all_gather(forcing, "z", axis=0, tiled=True, axis_index_groups=BACKWARD).reshape(FAR, 2, 96, 256)
    half_spec = pl.BlockSpec((4, 2, 96, 256), lambda step: (lax.rem(step, 2), 0, 0, 0))
    turned_spec = pl.BlockSpec((4, 2, 96, 256), lambda step: (1 - lax.rem(step, 2), 0, 0, 0))

    keep, give = pl.pallas_call(
        backward_kernel,
        grid=(4,),
        in_specs=[rows_of(4, 384, 128), rows_of(2, 384, 128), rows_of(2, 384, 128)]
        + [turned_spec, whole(64, 128), half_spec],
        out_specs=[whole(128, 2048)] * 2,
        out_shape=[shape_of((128, 2048), F32), shape_of((128, 2048))],
        scratch_shapes=[pltpu.VMEM((PAIR, 512, 256), F32)],
        compiler_params=params,
    )(own, first, second, forcing, lat_basis, lon)
    got = lax.ppermute(give, "core", SWAP)
    back = pl.pallas_call(add_kernel, out_shape=shape_of((128, 2048)), compiler_params=params)(keep, got)
    back = lax.all_to_all(back, ("pair", "chip"), 0, 0, tiled=True)
    gradient = pl.pallas_call(
        lambda *refs: gradient_kernel(factor, *refs),
        out_shape=shape_of((64, 256), F32),
        compiler_params=params,
    )(back, control.reshape(64, 256))
    return (increment.reshape(innovation.shape), gradient.reshape(control.shape))


def solution(mesh):
    members, space = ("z", "pair"), ("chip", "core")
    devices = mesh.devices.reshape(RING, PAIR, CHIPS, CORES)
    return jax.shard_map(
        per_device,
        mesh=Mesh(devices, (*members, *space)),
        in_specs=(
            P(members, None, None, space, None),
            P(members, None, None, space, None),
            P(space, None),
            P(members, None),
            P(None, None, space, members),
            P(None, None, space, members),
        ),
        out_specs=(P(None, None, space, members), P(members, None, None, space, None)),
        check_vma=False,
    )
```
